128 devices in a mesh: weight: 16 (over z, x_hi, core), context: 2 (over x_lo), tensor: 4 (over y).
Axes of the slice: x: 4 (x_hi: 2, x_lo: 2; x = x_hi * 2 + x_lo), y: 4, z: 4, core: 2. Of those that a mesh axis runs over, the one named last changes fastest.
Arguments:
- layer_input: bfloat16 [16384, 1152], P(('weight', 'context')), may hold values from -6 to 6
- positions: int32 [16384], P(('weight', 'context')), may hold values from 0 to 1023, as said below
- query_proj: bfloat16 [1152, 1024], P('weight', 'tensor'), may hold values from -0.1875 to 0.1875
- key_proj: bfloat16 [1152, 256], P('weight'), may hold values from -0.1875 to 0.1875
- value_proj: bfloat16 [1152, 256], P('weight'), may hold values from -0.1875 to 0.1875
- mixer_proj: bfloat16 [1024, 1152], P('tensor', 'weight'), may hold values from -0.1875 to 0.1875
- gate_proj: bfloat16 [1152, 6912], P('weight', 'tensor'), may hold values from -0.1875 to 0.1875
- up_proj: bfloat16 [1152, 6912], P('weight', 'tensor'), may hold values from -0.1875 to 0.1875
- down_proj: bfloat16 [6912, 1152], P('tensor', 'weight'), may hold values from -0.078125 to 0.078125
- input_gain: bfloat16 [1152], P('weight'), may hold values from 0.5 to 1.5
- query_gain: bfloat16 [256], P('weight'), may hold values from 0.5 to 1.5
- key_gain: bfloat16 [256], P('weight'), may hold values from 0.5 to 1.5
- mixer_gain: bfloat16 [1152], P('weight'), may hold values from 0.5 to 1.5
- middle_gain: bfloat16 [1152], P('weight'), may hold values from 0.5 to 1.5
- output_gain: bfloat16 [1152], P('weight'), may hold values from 0.5 to 1.5
- cotangent: bfloat16 [16384, 1152], P(('weight', 'context')), may hold values from -6 to 6
Outputs:
- output: bfloat16 [16384, 1152], P(('weight', 'context'))
- grad_input: float32 [16384, 1152], P(('weight', 'context'))
- query_grad: float32 [1152, 1024], P(('weight', 'context'), 'tensor')
- key_grad: float32 [1152, 256], P(('weight', 'context', 'tensor'))
- value_grad: float32 [1152, 256], P(('weight', 'context', 'tensor'))
- mixer_grad: float32 [1024, 1152], P('tensor', ('weight', 'context'))
- gate_grad: float32 [1152, 6912], P(('weight', 'context'), 'tensor')
- up_grad: float32 [1152, 6912], P(('weight', 'context'), 'tensor')
- down_grad: float32 [6912, 1152], P('tensor', ('weight', 'context'))
- input_gain_grad: float32 [1152], P(('weight', 'context'))
- query_gain_grad: float32 [256], P(('weight', 'context', 'tensor'))
- key_gain_grad: float32 [256], P(('weight', 'context', 'tensor'))
- mixer_gain_grad: float32 [1152], P(('weight', 'context'))
- middle_gain_grad: float32 [1152], P(('weight', 'context'))
- output_gain_grad: float32 [1152], P(('weight', 'context'))
The draws below stay inside these ranges and needn't reach their ends.
Inputs may be any that keep to these rules, and one draw needn't show every extreme that they name: The rows of each sequence (1024 rows, sequence after sequence) hold a permutation of 0 to 1023 made of runs of 256 consecutive increasing positions, each run starting at a multiple of 256; which run stands where is drawn for each sequence.
All inputs are finite; a program needn't handle non-finite values.
Results may differ from the reference program's by a relative error of at most 0.034.
Values may be sent and summed in bfloat16 or wider, within the bound.
No kernel may reach another device: no remote copies, remote signals or barrier semaphores. Data moves between devices by JAX's collectives and lax.ppermute only.
A program may use at most 128 MiB of HBM per device.

```python
import jax
import jax.numpy as jnp
from jax import lax

D = 1152
NH = 4
HD = 256
FF = 6912
SEQ_LEN = 1024
BLOCK = 256
SEQS = 16
TOKENS = 16384


def draw_positions(key, part):
    key = jax.random.fold_in(key, 11)
    block_count = SEQ_LEN // BLOCK
    seq_keys = jax.random.split(key, SEQS)
    orders = jax.vmap(lambda one_key: jax.random.permutation(one_key, block_count))(seq_keys)
    within = jnp.arange(BLOCK, dtype=jnp.int32)
    places = orders[:, :, None].astype(jnp.int32) * BLOCK + within[None, None, :]
    return places.reshape(SEQS * SEQ_LEN).astype(jnp.int32)


def block_levels(stream_key, dims, cuts, least, high):
    level = 1.0
    for dim, shards_of in cuts:
        draws = jax.random.uniform(jax.random.fold_in(jax.random.fold_in(stream_key, 6), dim), (shards_of,), jnp.float32, least / len(cuts), high / len(cuts))
        level = level * jnp.repeat(jnp.exp(draws), dims[dim] // shards_of).reshape((-1,) + (1,) * (len(dims) - 1 - dim))
    return level


def gaussian(stream_key, shape, scale, most, cuts=(), kind=jnp.bfloat16):
    values = jax.random.normal(stream_key, shape, jnp.float32) * scale
    if len(cuts) > 0:
        values = block_levels(stream_key, shape, cuts, -0.22, 0.18) * values
    return jnp.clip(values, min=-most, max=most).astype(kind)


def setup_inputs(seed: int = 0) -> dict:
    streams_of = jax.random.split(jax.random.key(seed), 17)
    return {
        "layer_input": gaussian(streams_of[0], (TOKENS, D), 1.0, 6.0, ((0, 32),)),
        "positions": draw_positions(jax.random.fold_in(streams_of[16], 71), 0),
        "query_proj": gaussian(streams_of[2], (D, NH * HD), D ** -0.5, 0.1875, ((0, 16), (1, 4))),
        "key_proj": gaussian(streams_of[3], (D, HD), D ** -0.5, 0.1875, ((0, 16),)),
        "value_proj": gaussian(streams_of[4], (D, HD), D ** -0.5, 0.1875, ((0, 16),)),
        "mixer_proj": gaussian(streams_of[5], (NH * HD, D), (NH * HD) ** -0.5, 0.1875, ((0, 4), (1, 16))),
        "gate_proj": gaussian(streams_of[6], (D, FF), D ** -0.5, 0.1875, ((0, 16), (1, 4))),
        "up_proj": gaussian(streams_of[7], (D, FF), D ** -0.5, 0.1875, ((0, 16), (1, 4))),
        "down_proj": gaussian(streams_of[8], (FF, D), FF ** -0.5, 0.078125, ((0, 4), (1, 16))),
        "input_gain": jnp.clip(1.0 + 0.1 * jax.random.normal(streams_of[9], (D,), jnp.float32), 0.5, 1.5).astype(jnp.bfloat16),
        "query_gain": jnp.clip(1.0 + 0.1 * jax.random.normal(streams_of[10], (HD,), jnp.float32), 0.5, 1.5).astype(jnp.bfloat16),
        "key_gain": jnp.clip(1.0 + 0.1 * jax.random.normal(streams_of[11], (HD,), jnp.float32), 0.5, 1.5).astype(jnp.bfloat16),
        "mixer_gain": jnp.clip(1.0 + 0.1 * jax.random.normal(streams_of[12], (D,), jnp.float32), 0.5, 1.5).astype(jnp.bfloat16),
        "middle_gain": jnp.clip(1.0 + 0.1 * jax.random.normal(streams_of[13], (D,), jnp.float32), 0.5, 1.5).astype(jnp.bfloat16),
        "output_gain": jnp.clip(1.0 + 0.1 * jax.random.normal(streams_of[14], (D,), jnp.float32), 0.5, 1.5).astype(jnp.bfloat16),
        "cotangent": gaussian(streams_of[15], (TOKENS, D), 1.0, 6.0, ((0, 32),)),
    }


@jax.custom_vjp
def low(v):
    return lax.optimization_barrier(v.astype(jnp.bfloat16)).astype(jnp.float32)

@jax.custom_vjp
def low_back(v):
    return v

def low_keep(v):
    return (low(v), None)

def low_pass(kept, grad):
    return (grad,)

def back_keep(v):
    return (v, None)

def back_low(kept, grad):
    return (low(grad),)
low.defvjp(low_keep, low_pass)
low_back.defvjp(back_keep, back_low)
EPSILON = 1e-06
ROPE_BASE = 1000000.0
NEGATIVE = -1e+30

def normed(values, gain_vec):
    factor = lax.rsqrt(lax.optimization_barrier(jnp.mean(values * values, axis=-1, keepdims=True)) + EPSILON)
    return values * factor * gain_vec

def angles_of(places, width):
    freq_index = jnp.arange(width // 2, dtype=jnp.float32)
    inverse = ROPE_BASE ** (-2.0 * freq_index / width)
    return places.astype(jnp.float32)[:, None] * inverse[None, :]

def rotated(values, angles):
    half_dim = values.shape[-1] // 2
    first_half = values[..., :half_dim]
    second_half = values[..., half_dim:]
    cosine = jnp.cos(angles)
    sine_val = jnp.sin(angles)
    return jnp.concatenate([first_half * cosine - second_half * sine_val, second_half * cosine + first_half * sine_val], axis=-1)

def matmul(left, right):
    return jnp.dot(left, right, precision=lax.Precision.HIGHEST, preferred_element_type=jnp.float32)

def sequence_layer(seq_rows, seq_places, weights):
    w_query, w_key, w_value, w_mixer, w_gate, w_up, w_down, gain_in, gain_query, gain_key, gain_mixer, gain_middle, gain_output = weights
    angles = angles_of(seq_places, HD)
    normed_in = low(normed(seq_rows, gain_in))
    query_raw = low_back(matmul(normed_in, w_query)).reshape(SEQ_LEN, NH, HD).transpose(1, 0, 2)
    key_raw = low_back(matmul(normed_in, w_key))
    value_low = low(low_back(matmul(normed_in, w_value)))
    query_low = low(rotated(normed(query_raw, gain_query), angles))
    key_low = low(rotated(normed(key_raw, gain_key), angles))
    scores = jnp.einsum('hqd,kd->hqk', query_low, key_low, precision=lax.Precision.HIGHEST) * HD ** (-0.5)
    scores = low_back(scores)
    visible = seq_places[None, :] <= seq_places[:, None]
    scores = jnp.where(visible[None], scores, NEGATIVE)
    row_max = lax.optimization_barrier(jnp.max(scores, axis=-1, keepdims=True))
    row_exp = jnp.exp(scores - row_max)
    probs_low = low(row_exp / lax.optimization_barrier(jnp.sum(row_exp, axis=-1, keepdims=True)))
    mixed_heads = jnp.einsum('hqk,kd->qhd', probs_low, value_low, precision=lax.Precision.HIGHEST)
    mixed_low = low(low_back(mixed_heads.reshape(SEQ_LEN, NH * HD)))
    mixer_sum = low_back(matmul(mixed_low, w_mixer))
    hidden_state = seq_rows + normed(mixer_sum, gain_mixer)
    middle_low = low(normed(hidden_state, gain_middle))
    gate_act = low_back(matmul(middle_low, w_gate))
    up_act = low_back(matmul(middle_low, w_up))
    inner_low = low(jax.nn.gelu(gate_act, approximate=True) * up_act)
    ffn_sum = low_back(matmul(inner_low, w_down))
    return hidden_state + normed(ffn_sum, gain_output)

def reference(layer_input, positions, query_proj, key_proj, value_proj, mixer_proj, gate_proj, up_proj, down_proj, input_gain, query_gain, key_gain, mixer_gain, middle_gain, output_gain, cotangent):
    params = tuple((item.astype(jnp.float32) for item in (query_proj, key_proj, value_proj, mixer_proj, gate_proj, up_proj, down_proj, input_gain, query_gain, key_gain, mixer_gain, middle_gain, output_gain)))
    residual = layer_input.astype(jnp.float32).reshape(SEQS, SEQ_LEN, D)
    places = positions.reshape(SEQS, SEQ_LEN).astype(jnp.int32)

    def forward(rows_all, weights):

        def one_sequence(seq_rows, seq_places):
            return sequence_layer(seq_rows, seq_places, weights)
        checked = jax.checkpoint(one_sequence)
        return lax.map(lambda pair: checked(pair[0], pair[1]), (rows_all, places))
    result, pull = jax.vjp(forward, residual, params)
    grad_rows, grads = pull(cotangent.astype(jnp.float32).reshape(SEQS, SEQ_LEN, D))
    return (result.reshape(TOKENS, D).astype(jnp.bfloat16), grad_rows.reshape(TOKENS, D), grads[0], grads[1], grads[2], grads[3], grads[4], grads[5], grads[6], grads[7], grads[8], grads[9], grads[10], grads[11], grads[12])
```

```python
import jax
import jax.numpy as jnp
from jax import lax
from jax.experimental import pallas as pl
from jax.experimental.pallas import tpu as pltpu
from jax.sharding import PartitionSpec as P

EPSILON = 1e-06
ROPE_BASE = 1000000.0
NEGATIVE = -1e30


def normed(values, gain_vec):
    factor = lax.rsqrt(jnp.mean(values * values, axis=-1, keepdims=True) + EPSILON)
    return values * factor * gain_vec


def angles_of(places, width):
    freq_index = jnp.arange(width // 2, dtype=jnp.float32)
    inverse = ROPE_BASE ** (-2.0 * freq_index / width)
    return places.astype(jnp.float32)[:, None] * inverse[None, :]


def rotated(values, angles):
    half_dim = values.shape[-1] // 2
    first_half = values[..., :half_dim]
    second_half = values[..., half_dim:]
    cosine = jnp.cos(angles)
    sine_val = jnp.sin(angles)
    return jnp.concatenate(
        [
            first_half * cosine - second_half * sine_val,
            second_half * cosine + first_half * sine_val,
        ],
        axis=-1,
    )


def gated(gate_in, up_in):
    return jax.nn.gelu(gate_in, approximate=True) * up_in


def matmul(left, right):
    return jnp.dot(left, right, preferred_element_type=jnp.float32)


def matmul_tn(left, right):
    return lax.dot_general(
        left, right, (((0,), (0,)), ((), ())), preferred_element_type=jnp.float32
    )


def matmul_nt(left, right):
    return lax.dot_general(
        left, right, (((1,), (1,)), ((), ())), preferred_element_type=jnp.float32
    )


SIXTEEN = range(16)


def to_core(values):
    return lax.ppermute(values, "weight", [(i, i ^ 1) for i in SIXTEEN])


def along_z(values, step):
    return lax.ppermute(values, "weight", [(i, (i + 4 * step) % 16) for i in SIXTEEN])


def along_x(values, step):
    pairs = []
    for i in range(32):
        place = 2 * ((i >> 2) & 1) + (i & 1)
        other = (place + step) % 4
        pairs.append((i, (i & 0b11010) | ((other >> 1) << 2) | (other & 1)))
    return lax.ppermute(values, ("weight", "context"), pairs)


def flipped(values):
    return lax.ppermute(values, ("weight", "context"), [(i, i ^ 5) for i in range(32)])


def to_context(values):
    return lax.ppermute(values, "context", [(0, 1), (1, 0)])


def along_y(values, step):
    return lax.ppermute(values, "tensor", [(i, (i + step) % 4) for i in range(4)])


STEPS = (1, 3, 2)


def after(values, *others):
    return lax.optimization_barrier((values,) + others)[0]


def pick(values, index, axis=0):
    return lax.dynamic_index_in_dim(values, index, axis, keepdims=False)


def ring_pieces(shard, move):
    moved = {step: move(shard, step) for step in STEPS}
    return [shard, moved[1], moved[2], moved[3]]


def in_places(pieces, place):
    whole = jnp.zeros((4,) + pieces[0].shape, pieces[0].dtype)
    for k in range(4):
        whole = lax.dynamic_update_index_in_dim(whole, pieces[k], (place - k) % 4, 0)
    return whole


def ring_gather(shard, place, move):
    return in_places(ring_pieces(shard, move), place)


def ring_sent(choose, place, move):
    return [move(choose((place + step) % 4), step) for step in STEPS]


def ring_total(own, moved):
    total = own.astype(jnp.float32)
    for piece in moved:
        total = total + piece.astype(jnp.float32)
    return total


def tensor_sum(partial, tensor, between=(), behind=()):
    rows, width = partial.shape
    chunks = partial.reshape(4, rows // 4, width)
    moved = ring_sent(lambda i: pick(chunks, i), tensor, along_y)
    if between:
        moved = [after(piece, *between) for piece in moved]
    share = ring_total(pick(chunks, tensor), moved).astype(jnp.bfloat16)
    pieces = ring_pieces(share, along_y)
    if behind:
        pieces = pieces[:1] + [after(piece, *behind) for piece in pieces[1:]]
    return in_places(pieces, tensor).reshape(rows, width)


def assembled(places, pieces, plan, columns):
    lead = pieces[0].shape[-2]
    count = len(plan) * len(columns)

    def kernel(places_ref, *refs):
        sources = refs[: len(pieces)]
        targets = refs[len(pieces) : len(pieces) + len(columns)]
        sems = refs[-1]
        copies = []
        for number, (piece, index, place) in enumerate(plan):
            for out, (low, high) in enumerate(columns):
                source = sources[piece].at[index]
                if len(columns) > 1:
                    source = source.at[:, pl.ds(low, high - low)]
                copies.append(
                    pltpu.make_async_copy(
                        source,
                        targets[out].at[places_ref[place]],
                        sems.at[number * len(columns) + out],
                    )
                )
        for copy in copies:
            copy.start()
        for copy in copies:
            copy.wait()

    total = sum(2 * piece.size * piece.dtype.itemsize for piece in pieces)
    outs = pl.pallas_call(
        kernel,
        out_shape=[
            jax.ShapeDtypeStruct((16, lead, high - low), pieces[0].dtype) for low, high in columns
        ],
        in_specs=[pl.BlockSpec(memory_space=pltpu.SMEM)]
        + [pl.BlockSpec(memory_space=pl.ANY)] * len(pieces),
        out_specs=[pl.BlockSpec(memory_space=pltpu.VMEM)] * len(columns),
        compiler_params=pltpu.CompilerParams(vmem_limit_bytes=24 * 1024 * 1024),
        scratch_shapes=[pltpu.SemaphoreType.DMA((count,))],
        cost_estimate=pl.CostEstimate(flops=0, bytes_accessed=total, transcendentals=0),
        name="assembled",
    )(places, *pieces)
    return [out.reshape(16 * lead, out.shape[2]) for out in outs]


def chip_halves(left, core):
    blocks = left.T.reshape(8, 2, 72, left.shape[0])
    return [pick(blocks, which, 1).reshape(576, -1) for which in (1 - core, core)]


def window(values, place):
    lead = values.ndim - 3
    start = (0,) * lead + (place // 2, 32 * (place % 2), 0)
    out = lax.dynamic_slice(values, start, values.shape[:lead] + (1, 40, values.shape[-1]))
    return out.reshape(values.shape[:lead] + (40, values.shape[-1]))


def ring_one(half, order, z, x):
    half = half.reshape(4, 2, 72, half.shape[1])
    choose = (lambda i: pick(half, i)) if order == "zx" else (lambda i: window(half, i))
    place, move = (z, along_z) if order == "zx" else (x, along_x)
    return choose(place), ring_sent(choose, place, move)


def ring_two(part, order, z, x, x_lo):
    choose = (lambda i: window(part, i)) if order == "zx" else (lambda i: pick(part, i))
    place, move = (x, along_x) if order == "zx" else (z, along_z)
    done = ring_total(choose(place), ring_sent(choose, place, move))
    return lax.dynamic_slice(done, (4 * x_lo, 0), (36, done.shape[1]))


def local(
    layer_input,
    positions,
    query_proj,
    key_proj,
    value_proj,
    mixer_proj,
    gate_proj,
    up_proj,
    down_proj,
    input_gain,
    query_gain,
    key_gain,
    mixer_gain,
    middle_gain,
    output_gain,
    cotangent,
):
    bf16, f32 = jnp.bfloat16, jnp.float32
    weight = lax.axis_index("weight")
    z, x_hi, core = weight // 4, (weight // 2) % 2, weight % 2
    x_lo = lax.axis_index("context")
    tensor = lax.axis_index("tensor")
    x = 2 * x_hi + x_lo
    rows, width = layer_input.shape
    head_dim = key_proj.shape[1]
    hidden = gate_proj.shape[1]
    padded = -(-hidden // 128) * 128
    score_scale = head_dim ** (-0.5)

    back = (z - jnp.arange(4, dtype=jnp.int32)) % 4
    sides = []
    for x_there in (x_hi, 1 - x_hi):
        for core_there in (core, 1 - core):
            sides.append(4 * back + 2 * x_there + core_there)
    places = jnp.concatenate(sides).astype(jnp.int32)

    gain_rows = [input_gain, mixer_gain, middle_gain, output_gain, query_gain, key_gain]
    gain_rows = [jnp.pad(g, (0, 3 * head_dim - g.shape[0])) for g in gain_rows]
    gain_rows = jnp.stack(gain_rows + gain_rows[:2])
    first = jnp.concatenate([query_proj, key_proj, value_proj], axis=1)
    first = jnp.concatenate([first, gain_rows], axis=0)
    here = jnp.stack(ring_pieces(first, along_z))
    other_input = to_context(layer_input)
    other_places = to_context(positions)
    there = flipped(here)
    near = jnp.stack([here, there])
    across = to_core(near)
    plan = []
    for piece in (0, 1):
        for side in (0, 1):
            for k in range(4):
                plan.append((piece, (side, k), 4 * (2 * side + piece) + k))
    (first_all,) = assembled(places, [near, across], plan, [(0, 3 * head_dim)])
    first_all = first_all.reshape(16, 80, 3 * head_dim)
    w_qkv = first_all[:, :72].reshape(width, 3 * head_dim)
    gain_all = first_all[:, 72:]

    def wide_gain(i):
        return gain_all[:, i, :72].reshape(width).astype(f32)

    gain_in, gain_mixer, gain_middle, gain_output = (wide_gain(i) for i in range(4))
    gain_query = gain_all[:, 4, :16].reshape(head_dim).astype(f32)
    gain_key = gain_all[:, 5, :16].reshape(head_dim).astype(f32)

    fill = ((0, 0), (0, padded - hidden))
    wide = jnp.concatenate([jnp.pad(gate_proj, fill), jnp.pad(up_proj, fill)], axis=1)
    wide_z = ring_pieces(after(wide, here), along_z)
    wide_z = wide_z[:1] + [after(piece, first_all) for piece in wide_z[1:]]
    wide_f = [flipped(after(wide, there))] + [flipped(piece) for piece in wide_z[1:]]

    mixer_pieces = ring_pieces(after(mixer_proj, here).T, along_y)
    mixer_rows = in_places([after(piece, first_all) for piece in mixer_pieces], tensor)
    mixer_rows = mixer_rows.transpose(1, 0, 2).reshape(72, 4 * head_dim)
    last = jnp.concatenate([jnp.pad(down_proj.T, fill), mixer_rows], axis=1)
    last_z = ring_pieces(jnp.stack([last, flipped(last)]), along_z)

    residual = layer_input.astype(f32)
    normed_f, input_pull = jax.vjp(normed, residual, gain_in)
    normed_in = normed_f.astype(bf16)
    normed_other = normed(other_input.astype(f32), gain_in).astype(bf16)
    normed_all = jnp.concatenate([normed_in, normed_other], axis=0)
    query_raw = matmul(normed_in, w_qkv[:, :head_dim])
    kv_raw = matmul(normed_all, w_qkv[:, head_dim:])
    key_raw = kv_raw[:, :head_dim]
    value_all = kv_raw[:, head_dim:].astype(bf16)
    key_places = jnp.concatenate([positions, other_places])
    angles_all = angles_of(key_places, head_dim)
    angles = angles_all[:rows]

    def query_shape(raw_rows, gain_vec):
        return rotated(normed(raw_rows, gain_vec), angles)

    query_rot, query_pull = jax.vjp(query_shape, query_raw, gain_query)
    query_low = query_rot.astype(bf16)
    key_all = rotated(normed(key_raw, gain_key), angles_all).astype(bf16)
    visible = key_places[None, :] <= positions[:, None]

    def score_block():
        return jnp.where(visible, matmul_nt(query_low, key_all) * score_scale, NEGATIVE)

    scores = after(score_block(), wide_f[0], wide_f[1], last_z[1])
    row_max = jnp.max(scores, axis=-1, keepdims=True)
    row_exp = jnp.exp(scores - row_max)
    row_total = jnp.sum(row_exp, axis=-1, keepdims=True)
    log_total = row_max + jnp.log(row_total)
    probs_low = after((row_exp / row_total).astype(bf16), wide_f[2], last_z[3])
    mixed_low = matmul(probs_low, value_all).astype(bf16)

    mixed_pieces = ring_pieces(mixed_low, along_y)
    mixed_pieces[2] = after(mixed_pieces[2], wide_f[3], last_z[2])
    mixed_all = in_places(mixed_pieces, tensor)
    mixed_all = mixed_all.transpose(1, 0, 2).reshape(rows, 4 * head_dim)
    last_pieces = last_z + [to_core(piece) for piece in last_z]
    wide_near = wide_z + wide_f
    wide_pieces = [piece[None] for piece in wide_near + [to_core(piece) for piece in wide_near]]
    last_plan, wide_plan = [], []
    for piece in (0, 1):
        for side in (0, 1):
            for k in range(4):
                place = 4 * (2 * side + piece) + k
                last_plan.append((4 * piece + k, side, place))
                wide_plan.append((8 * piece + 4 * side + k, 0, place))
    w_down, w_mixer = assembled(
        places, last_pieces, last_plan, [(0, padded), (padded, padded + 4 * head_dim)]
    )
    (w_wide,) = assembled(places, wide_pieces, wide_plan, [(0, 2 * padded)])
    mixer_sum = matmul_nt(mixed_all, w_mixer)
    mixer_normed, mixer_pull = jax.vjp(normed, mixer_sum, gain_mixer)
    hidden_state = residual + mixer_normed
    middle_normed, middle_pull = jax.vjp(normed, hidden_state, gain_middle)
    middle_low = middle_normed.astype(bf16)
    wide_act = matmul(middle_low, w_wide)
    inner_act, inner_pull = jax.vjp(gated, wide_act[:, :padded], wide_act[:, padded:])
    inner_low = inner_act.astype(bf16)
    ffn_part = matmul_nt(inner_low, w_down).astype(bf16)
    middle_sent, middle_kept = chip_halves(after(middle_low, ffn_part), core)
    normed_sent, normed_kept = chip_halves(after(normed_in, ffn_part), core)
    ffn_sum = tensor_sum(
        ffn_part, tensor, (middle_sent, middle_kept), (normed_sent, normed_kept)
    ).astype(f32)
    ffn_normed, ffn_pull = jax.vjp(normed, ffn_sum, gain_output)
    output = (hidden_state + ffn_normed).astype(bf16)
    grad_out = cotangent.astype(f32)
    grad_ffn, grad_gain_output = ffn_pull(grad_out)
    grad_ffn_low = grad_ffn.astype(bf16)

    grad_inner = matmul(grad_ffn_low, w_down)
    grad_gate, grad_up = inner_pull(grad_inner)
    grad_wide_low = jnp.concatenate([grad_gate.astype(bf16), grad_up.astype(bf16)], axis=1)
    middle_part = matmul_nt(grad_wide_low, w_wide).astype(bf16)
    wide_sent = matmul(after(middle_sent, middle_part), grad_wide_low).astype(bf16)
    wide_came = to_core(wide_sent)
    ffn_sent, ffn_kept = chip_halves(after(grad_ffn_low, middle_part), core)
    down_sent = matmul(ffn_sent, inner_low).astype(bf16)
    down_came = to_core(down_sent)
    wide_half = (matmul(middle_kept, grad_wide_low) + wide_came.astype(f32)).astype(bf16)
    wide_own, wide_ring = ring_one(wide_half, "zx", z, x)
    down_half = (matmul(ffn_kept, inner_low) + down_came.astype(f32)).astype(bf16)
    down_own, down_ring = ring_one(down_half, "xz", z, x)
    grad_middle = tensor_sum(
        middle_part, tensor, (wide_sent, down_sent), (wide_half, down_half)
    ).astype(f32)

    grad_hidden_norm, grad_gain_middle = middle_pull(grad_middle)
    grad_hidden = grad_out + grad_hidden_norm
    grad_mixer, grad_gain_mixer = mixer_pull(grad_hidden)
    grad_mixer_low = grad_mixer.astype(bf16)
    w_mixer_own = lax.dynamic_slice_in_dim(w_mixer, tensor * head_dim, head_dim, 1)
    grad_mixed_low = matmul(grad_mixer_low, w_mixer_own).astype(bf16)

    attn_probs = jnp.exp(score_block() - log_total)
    probs_again = attn_probs.astype(bf16)
    grad_probs = matmul_nt(grad_mixed_low, value_all)
    grad_scores = attn_probs * (
        grad_probs - jnp.sum(attn_probs * grad_probs, axis=-1, keepdims=True)
    )
    grad_scores_low = grad_scores.astype(bf16)
    grad_key_part = matmul_tn(grad_scores_low, query_low) * score_scale
    grad_value_part = matmul_tn(probs_again, grad_mixed_low)
    grad_kv = jnp.concatenate([grad_key_part, grad_value_part], axis=1)
    to_other = grad_kv[rows:].astype(bf16)
    from_other = to_context(to_other)
    grad_query_rot = matmul(grad_scores_low, key_all) * score_scale
    grad_query_raw, grad_gain_query = query_pull(grad_query_rot)
    grad_kv = grad_kv[:rows] + from_other.astype(f32)

    def key_shape(raw_rows, gain_vec):
        return rotated(normed(raw_rows, gain_vec), angles)

    key_unused, key_pull = jax.vjp(key_shape, key_raw[:rows], gain_key)
    grad_key_raw, grad_gain_key = key_pull(grad_kv[:, :head_dim])
    grad_qkv_low = jnp.concatenate(
        [grad_query_raw, grad_key_raw, grad_kv[:, head_dim:]], axis=1
    ).astype(bf16)
    input_part = matmul_nt(grad_qkv_low, w_qkv)
    unused, grad_gain_in = input_pull(input_part)
    def narrow(vec):
        return jnp.pad(vec.reshape(32, 8), ((0, 0), (0, 28))).reshape(width)

    columns = jnp.stack(
        [
            grad_gain_in,
            narrow(grad_gain_query),
            narrow(grad_gain_key),
            grad_gain_mixer * 0.25,
            grad_gain_middle * 0.25,
            grad_gain_output * 0.25,
        ]
    )
    columns = jnp.pad(columns, ((0, 128 - 6), (0, 0)))
    input_low = input_part.astype(bf16)
    mixer_sent, mixer_kept = chip_halves(grad_mixer_low, core)
    column_sent, column_kept = chip_halves(columns, core)

    def small_half(normed_rows, column_rows, mixer_rows):
        parts = [matmul(normed_rows, grad_qkv_low), column_rows, matmul(mixer_rows, mixed_low)]
        return jnp.concatenate(parts, axis=1)

    small_sent = small_half(normed_sent, column_sent, mixer_sent).astype(bf16)
    small_came = to_core(small_sent)
    small_own = small_half(normed_kept, column_kept, mixer_kept)
    small_half_sum = (small_own + small_came.astype(f32)).astype(bf16)
    small_ring_own, small_ring = ring_one(small_half_sum, "xz", z, x)
    wide_part = ring_total(wide_own, [after(p, to_other) for p in wide_ring]).astype(bf16)
    down_part = ring_total(down_own, [after(p, to_other) for p in down_ring]).astype(bf16)
    grad_normed = tensor_sum(
        input_low, tensor, (small_sent,), (small_half_sum, wide_part, down_part)
    ).astype(f32)
    small = ring_two(ring_total(small_ring_own, small_ring).astype(bf16), "xz", z, x, x_lo)
    wide_out = ring_two(wide_part, "zx", z, x, x_lo)
    down_out = ring_two(down_part, "xz", z, x, x_lo)[:, :hidden].T
    gate_out, up_out = wide_out[:, :hidden], wide_out[:, padded : padded + hidden]
    query_out = small[:, :head_dim]
    shared = small[:, head_dim : 3 * head_dim + 128]
    mixer_out = small[:, 3 * head_dim + 128 :].T
    shared_low = jnp.pad(shared, ((0, 4), (0, 0))).astype(bf16)
    for piece in [along_y(shared_low, step) for step in STEPS]:
        shared = shared + piece[:36].astype(f32)
    kv_out = lax.dynamic_slice_in_dim(shared[:, : 2 * head_dim], 9 * tensor, 9, 0)
    key_out, value_out = kv_out[:, :head_dim], kv_out[:, head_dim:]
    gain_cols = shared[:, 2 * head_dim :]
    two = lax.dynamic_slice_in_dim(gain_cols, 2 * tensor, 2, 0)

    grad_resid_norm, unused_gain = input_pull(grad_normed)
    grad_input = grad_hidden + grad_resid_norm
    return (
        output,
        grad_input,
        query_out,
        key_out,
        value_out,
        mixer_out,
        gate_out,
        up_out,
        down_out,
        gain_cols[:, 0],
        two[:, 1],
        two[:, 2],
        gain_cols[:, 3],
        gain_cols[:, 4],
        gain_cols[:, 5],
    )


def solution(mesh):
    in_specs = (
        P(("weight", "context"), None),
        P(("weight", "context")),
        P("weight", "tensor"),
        P("weight", None),
        P("weight", None),
        P("tensor", "weight"),
        P("weight", "tensor"),
        P("weight", "tensor"),
        P("tensor", "weight"),
        P("weight"),
        P("weight"),
        P("weight"),
        P("weight"),
        P("weight"),
        P("weight"),
        P(("weight", "context"), None),
    )
    out_specs = (
        P(("weight", "context"), None),
        P(("weight", "context"), None),
        P(("weight", "context"), "tensor"),
        P(("weight", "context", "tensor"), None),
        P(("weight", "context", "tensor"), None),
        P("tensor", ("weight", "context")),
        P(("weight", "context"), "tensor"),
        P(("weight", "context"), "tensor"),
        P("tensor", ("weight", "context")),
        P(("weight", "context")),
        P(("weight", "context", "tensor")),
        P(("weight", "context", "tensor")),
        P(("weight", "context")),
        P(("weight", "context")),
        P(("weight", "context")),
    )
    return jax.shard_map(local, mesh=mesh, in_specs=in_specs, out_specs=out_specs, check_vma=False)
```

```python
import jax
import jax.numpy as jnp
from jax import lax
from jax.experimental import pallas as pl
from jax.experimental.pallas import tpu as pltpu
from jax.sharding import PartitionSpec as P

EPSILON = 1e-06
ROPE_BASE = 1000000.0
NEGATIVE = -1e30


def normed(values, gain_vec):
    factor = lax.rsqrt(jnp.mean(values * values, axis=-1, keepdims=True) + EPSILON)
    return values * factor * gain_vec


def angles_of(places, width):
    freq_index = jnp.arange(width // 2, dtype=jnp.float32)
    inverse = ROPE_BASE ** (-2.0 * freq_index / width)
    return places.astype(jnp.float32)[:, None] * inverse[None, :]


def rotated(values, angles):
    half_dim = values.shape[-1] // 2
    first_half = values[..., :half_dim]
    second_half = values[..., half_dim:]
    cosine = jnp.cos(angles)
    sine_val = jnp.sin(angles)
    return jnp.concatenate(
        [
            first_half * cosine - second_half * sine_val,
            second_half * cosine + first_half * sine_val,
        ],
        axis=-1,
    )


def gated(gate_in, up_in):
    return jax.nn.gelu(gate_in, approximate=True) * up_in


def matmul(left, right):
    return jnp.dot(left, right, preferred_element_type=jnp.float32)


def matmul_tn(left, right):
    return lax.dot_general(
        left, right, (((0,), (0,)), ((), ())), preferred_element_type=jnp.float32
    )


def matmul_nt(left, right):
    return lax.dot_general(
        left, right, (((1,), (1,)), ((), ())), preferred_element_type=jnp.float32
    )


SIXTEEN = range(16)


def to_core(values):
    return lax.ppermute(values, "weight", [(i, i ^ 1) for i in SIXTEEN])


def along_z(values, step):
    return lax.ppermute(values, "weight", [(i, (i + 4 * step) % 16) for i in SIXTEEN])


def along_x(values, step):
    pairs = []
    for i in range(32):
        place = 2 * ((i >> 2) & 1) + (i & 1)
        other = (place + step) % 4
        pairs.append((i, (i & 0b11010) | ((other >> 1) << 2) | (other & 1)))
    return lax.ppermute(values, ("weight", "context"), pairs)


def flipped(values):
    return lax.ppermute(values, ("weight", "context"), [(i, i ^ 5) for i in range(32)])


def to_context(values):
    return lax.ppermute(values, "context", [(0, 1), (1, 0)])


def along_y(values, step):
    return lax.ppermute(values, "tensor", [(i, (i + step) % 4) for i in range(4)])


STEPS = (1, 3, 2)


def after(values, *others):
    return lax.optimization_barrier((values,) + others)[0]


def pick(values, index, axis=0):
    return lax.dynamic_index_in_dim(values, index, axis, keepdims=False)


def ring_pieces(shard, move):
    moved = {step: move(shard, step) for step in STEPS}
    return [shard, moved[1], moved[2], moved[3]]


def in_places(pieces, place):
    whole = jnp.zeros((4,) + pieces[0].shape, pieces[0].dtype)
    for k in range(4):
        whole = lax.dynamic_update_index_in_dim(whole, pieces[k], (place - k) % 4, 0)
    return whole


def ring_gather(shard, place, move):
    return in_places(ring_pieces(shard, move), place)


def ring_sent(choose, place, move):
    return [move(choose((place + step) % 4), step) for step in STEPS]


def ring_total(own, moved):
    total = own.astype(jnp.float32)
    for piece in moved:
        total = total + piece.astype(jnp.float32)
    return total


def tensor_sum(partial, tensor, between=(), behind=()):
    rows, width = partial.shape
    chunks = partial.reshape(4, rows // 4, width)
    moved = ring_sent(lambda i: pick(chunks, i), tensor, along_y)
    if between:
        moved = [after(piece, *between) for piece in moved]
    share = ring_total(pick(chunks, tensor), moved).astype(jnp.bfloat16)
    pieces = ring_pieces(share, along_y)
    if behind:
        pieces = pieces[:1] + [after(piece, *behind) for piece in pieces[1:]]
    return in_places(pieces, tensor).reshape(rows, width)


def assembled(places, pieces, plan, columns):
    lead = pieces[0].shape[-2]
    count = len(plan) * len(columns)

    def kernel(places_ref, *refs):
        sources = refs[: len(pieces)]
        targets = refs[len(pieces) : len(pieces) + len(columns)]
        sems = refs[-1]
        copies = []
        for number, (piece, index, place) in enumerate(plan):
            for out, (low, high) in enumerate(columns):
                source = sources[piece].at[index]
                if len(columns) > 1:
                    source = source.at[:, pl.ds(low, high - low)]
                copies.append(
                    pltpu.make_async_copy(
                        source,
                        targets[out].at[places_ref[place]],
                        sems.at[number * len(columns) + out],
                    )
                )
        for copy in copies:
            copy.start()
        for copy in copies:
            copy.wait()

    total = sum(2 * piece.size * piece.dtype.itemsize for piece in pieces)
    outs = pl.pallas_call(
        kernel,
        out_shape=[
            jax.ShapeDtypeStruct((16, lead, high - low), pieces[0].dtype) for low, high in columns
        ],
        in_specs=[pl.BlockSpec(memory_space=pltpu.SMEM)]
        + [pl.BlockSpec(memory_space=pl.ANY)] * len(pieces),
        out_specs=[pl.BlockSpec(memory_space=pltpu.VMEM)] * len(columns),
        compiler_params=pltpu.CompilerParams(vmem_limit_bytes=24 * 1024 * 1024),
        scratch_shapes=[pltpu.SemaphoreType.DMA((count,))],
        cost_estimate=pl.CostEstimate(flops=0, bytes_accessed=total, transcendentals=0),
        name="assembled",
    )(places, *pieces)
    return [out.reshape(16 * lead, out.shape[2]) for out in outs]


def dot_of(left, right, left_dim, right_dim):
    dims = (((left_dim,), (right_dim,)), ((), ()))
    return lax.dot_general(left, right, dims, preferred_element_type=jnp.float32)


STRIP = 128


def block_scores(query, key, query_places, key_places):
    scores = dot_of(query, key, 1, 1) * (query.shape[1] ** (-0.5))
    return jnp.where(key_places <= query_places, scores, NEGATIVE)


def attend(query, key, value, query_places, key_places):
    rows, dim = query.shape

    def kernel(q_ref, k_ref, v_ref, qp_ref, kp_ref, out_ref, lse_ref):
        @pl.loop(0, rows // STRIP)
        def _(i):
            here = pl.ds(i * STRIP, STRIP)
            scores = block_scores(q_ref[here], k_ref[...], qp_ref[here], kp_ref[...])
            row_max = jnp.max(scores, axis=-1, keepdims=True)
            row_exp = jnp.exp(scores - row_max)
            row_total = jnp.sum(row_exp, axis=-1, keepdims=True)
            probs = (row_exp / row_total).astype(jnp.bfloat16)
            out_ref[here] = dot_of(probs, v_ref[...], 1, 0).astype(jnp.bfloat16)
            lse_ref[here] = row_max + jnp.log(row_total)

    vmem = pl.BlockSpec(memory_space=pltpu.VMEM)
    return pl.pallas_call(
        kernel,
        out_shape=[
            jax.ShapeDtypeStruct((rows, dim), jnp.bfloat16),
            jax.ShapeDtypeStruct((rows, 1), jnp.float32),
        ],
        in_specs=[vmem] * 5,
        out_specs=[vmem] * 2,
        compiler_params=pltpu.CompilerParams(vmem_limit_bytes=24 * 1024 * 1024),
        name="attend",
    )(query, key, value, query_places, key_places)


def attend_back(query, key, value, grad, lse, query_places, key_places):
    rows, dim = query.shape
    scale = dim ** (-0.5)

    def kernel(q_ref, k_ref, v_ref, g_ref, l_ref, qp_ref, kp_ref, gq_ref, own_ref, far_ref, sums):
        sums[...] = jnp.zeros_like(sums)

        @pl.loop(0, rows // STRIP)
        def _(i):
            here = pl.ds(i * STRIP, STRIP)
            query, grad = q_ref[here], g_ref[here]
            scores = block_scores(query, k_ref[...], qp_ref[here], kp_ref[...])
            probs = jnp.exp(scores - l_ref[here])
            grad_probs = dot_of(grad, v_ref[...], 1, 1)
            mean = jnp.sum(probs * grad_probs, axis=-1, keepdims=True)
            grad_scores = (probs * (grad_probs - mean)).astype(jnp.bfloat16)
            gq_ref[here] = dot_of(grad_scores, k_ref[...], 1, 0) * scale
            sums[:, :dim] += dot_of(grad_scores, query, 0, 0) * scale
            sums[:, dim:] += dot_of(probs.astype(jnp.bfloat16), grad, 0, 0)

        own_ref[...] = sums[:rows]
        far_ref[...] = sums[rows:].astype(jnp.bfloat16)

    vmem = pl.BlockSpec(memory_space=pltpu.VMEM)
    return pl.pallas_call(
        kernel,
        out_shape=[
            jax.ShapeDtypeStruct((rows, dim), jnp.float32),
            jax.ShapeDtypeStruct((rows, 2 * dim), jnp.float32),
            jax.ShapeDtypeStruct((key.shape[0] - rows, 2 * dim), jnp.bfloat16),
        ],
        in_specs=[vmem] * 7,
        out_specs=[vmem] * 3,
        scratch_shapes=[pltpu.VMEM((key.shape[0], 2 * dim), jnp.float32)],
        compiler_params=pltpu.CompilerParams(vmem_limit_bytes=32 * 1024 * 1024),
        name="attend_back",
    )(query, key, value, grad, lse, query_places, key_places)


def chip_halves(left, core):
    blocks = left.T.reshape(8, 2, 72, left.shape[0])
    return [pick(blocks, which, 1).reshape(576, -1) for which in (1 - core, core)]


def window(values, place):
    lead = values.ndim - 3
    start = (0,) * lead + (place // 2, 32 * (place % 2), 0)
    out = lax.dynamic_slice(values, start, values.shape[:lead] + (1, 40, values.shape[-1]))
    return out.reshape(values.shape[:lead] + (40, values.shape[-1]))


def ring_one(half, order, z, x):
    half = half.reshape(4, 2, 72, half.shape[1])
    choose = (lambda i: pick(half, i)) if order == "zx" else (lambda i: window(half, i))
    place, move = (z, along_z) if order == "zx" else (x, along_x)
    return choose(place), ring_sent(choose, place, move)


def ring_two(part, order, z, x):
    choose = (lambda i: window(part, i)) if order == "zx" else (lambda i: pick(part, i))
    place, move = (x, along_x) if order == "zx" else (z, along_z)
    return choose(place), ring_sent(choose, place, move)


def owned(own, moved, x_lo):
    return lax.dynamic_slice(ring_total(own, moved), (4 * x_lo, 0), (36, own.shape[1]))


def local(
    layer_input,
    positions,
    query_proj,
    key_proj,
    value_proj,
    mixer_proj,
    gate_proj,
    up_proj,
    down_proj,
    input_gain,
    query_gain,
    key_gain,
    mixer_gain,
    middle_gain,
    output_gain,
    cotangent,
):
    bf16, f32 = jnp.bfloat16, jnp.float32
    weight = lax.axis_index("weight")
    z, x_hi, core = weight // 4, (weight // 2) % 2, weight % 2
    x_lo = lax.axis_index("context")
    tensor = lax.axis_index("tensor")
    x = 2 * x_hi + x_lo
    rows, width = layer_input.shape
    head_dim = key_proj.shape[1]
    hidden = gate_proj.shape[1]
    padded = -(-hidden // 128) * 128

    back = (z - jnp.arange(4, dtype=jnp.int32)) % 4
    sides = []
    for x_there in (x_hi, 1 - x_hi):
        for core_there in (core, 1 - core):
            sides.append(4 * back + 2 * x_there + core_there)
    places = jnp.concatenate(sides).astype(jnp.int32)

    gain_rows = [input_gain, mixer_gain, middle_gain, output_gain, query_gain, key_gain]
    gain_rows = [jnp.pad(g, (0, 3 * head_dim - g.shape[0])) for g in gain_rows]
    gain_rows = jnp.stack(gain_rows + gain_rows[:2])
    first = jnp.concatenate([query_proj, key_proj, value_proj], axis=1)
    first = jnp.concatenate([first, gain_rows], axis=0)
    here = jnp.stack(ring_pieces(first, along_z))
    other_input = to_context(layer_input)
    other_places = to_context(positions)
    there = flipped(here)
    near = jnp.stack([here, there])
    across = to_core(near)
    plan = []
    for piece in (0, 1):
        for side in (0, 1):
            for k in range(4):
                plan.append((piece, (side, k), 4 * (2 * side + piece) + k))
    (first_all,) = assembled(places, [near, across], plan, [(0, 3 * head_dim)])
    first_all = first_all.reshape(16, 80, 3 * head_dim)
    w_qkv = first_all[:, :72].reshape(width, 3 * head_dim)
    gain_all = first_all[:, 72:]

    def wide_gain(i):
        return gain_all[:, i, :72].reshape(width).astype(f32)

    gain_in, gain_mixer, gain_middle, gain_output = (wide_gain(i) for i in range(4))
    gain_query = gain_all[:, 4, :16].reshape(head_dim).astype(f32)
    gain_key = gain_all[:, 5, :16].reshape(head_dim).astype(f32)

    fill = ((0, 0), (0, padded - hidden))
    wide = jnp.concatenate([jnp.pad(gate_proj, fill), jnp.pad(up_proj, fill)], axis=1)
    wide_z = ring_pieces(after(wide, here), along_z)
    wide_f = [flipped(after(wide, there))] + [flipped(piece) for piece in wide_z[1:]]

    mixer_pieces = ring_pieces(after(mixer_proj, here).T, along_y)
    last = jnp.concatenate([jnp.pad(down_proj.T, fill)] + mixer_pieces, axis=1)
    last_there = flipped(last)
    last_z = ring_pieces(jnp.stack([last, last_there]), along_z)

    residual = layer_input.astype(f32)
    normed_f, input_pull = jax.vjp(normed, residual, gain_in)
    normed_in = normed_f.astype(bf16)
    normed_other = normed(other_input.astype(f32), gain_in).astype(bf16)
    normed_all = jnp.concatenate([normed_in, normed_other], axis=0)
    normed_all = after(normed_all, *wide_z[1:], wide_f[0], last_there)
    query_raw = matmul(normed_all[:rows], w_qkv[:, :head_dim])
    kv_raw = matmul(normed_all, w_qkv[:, head_dim:])
    key_raw = kv_raw[:, :head_dim]
    value_all = kv_raw[:, head_dim:].astype(bf16)
    key_places = jnp.concatenate([positions, after(other_places, first_all)])
    angles_all = angles_of(key_places, head_dim)
    angles = angles_all[:rows]

    def query_shape(raw_rows, gain_vec):
        return rotated(normed(raw_rows, gain_vec), angles)

    query_rot, query_pull = jax.vjp(query_shape, query_raw, gain_query)
    query_low = query_rot.astype(bf16)
    key_all = rotated(normed(key_raw, gain_key), angles_all).astype(bf16)
    query_places, key_row = positions[:, None], key_places[None, :]
    mixed_low, log_total = attend(query_low, key_all, value_all, query_places, key_row)

    mixed_pieces = ring_pieces(mixed_low, along_y)
    wide_f = wide_f[:1] + [after(piece, mixed_low) for piece in wide_f[1:]]
    last_z = last_z[:1] + [after(piece, mixed_low) for piece in last_z[1:]]
    mixed_all = jnp.concatenate(mixed_pieces, axis=1)
    last_pieces = last_z + [to_core(piece) for piece in last_z]
    wide_near = wide_z + wide_f
    wide_pieces = [piece[None] for piece in wide_near + [to_core(piece) for piece in wide_near]]
    last_plan, wide_plan = [], []
    for piece in (0, 1):
        for side in (0, 1):
            for k in range(4):
                place = 4 * (2 * side + piece) + k
                last_plan.append((4 * piece + k, side, place))
                wide_plan.append((8 * piece + 4 * side + k, 0, place))
    w_down, w_mixer = assembled(
        places, last_pieces, last_plan, [(0, padded), (padded, padded + 4 * head_dim)]
    )
    (w_wide,) = assembled(places, wide_pieces, wide_plan, [(0, 2 * padded)])
    mixer_sum = matmul_nt(mixed_all, w_mixer)
    mixer_normed, mixer_pull = jax.vjp(normed, mixer_sum, gain_mixer)
    hidden_state = residual + mixer_normed
    middle_normed, middle_pull = jax.vjp(normed, hidden_state, gain_middle)
    middle_low = middle_normed.astype(bf16)
    wide_act = matmul(middle_low, w_wide)
    inner_act, inner_pull = jax.vjp(gated, wide_act[:, :padded], wide_act[:, padded:])
    inner_low = inner_act.astype(bf16)
    ffn_part = matmul_nt(inner_low, w_down).astype(bf16)
    middle_sent, middle_kept = chip_halves(after(middle_low, ffn_part), core)
    normed_sent, normed_kept = chip_halves(after(normed_in, ffn_part), core)
    ffn_sum = tensor_sum(
        ffn_part, tensor, (middle_sent, middle_kept), (normed_sent, normed_kept)
    ).astype(f32)
    ffn_normed, ffn_pull = jax.vjp(normed, ffn_sum, gain_output)
    output = (hidden_state + ffn_normed).astype(bf16)
    grad_out = cotangent.astype(f32)
    grad_ffn, grad_gain_output = ffn_pull(grad_out)
    grad_ffn_low = grad_ffn.astype(bf16)

    grad_inner = matmul(grad_ffn_low, w_down)
    grad_gate, grad_up = inner_pull(grad_inner)
    grad_wide_low = jnp.concatenate([grad_gate.astype(bf16), grad_up.astype(bf16)], axis=1)
    middle_part = matmul_nt(grad_wide_low, w_wide).astype(bf16)
    wide_sent = matmul(after(middle_sent, middle_part), grad_wide_low).astype(bf16)
    wide_came = to_core(wide_sent)
    ffn_sent, ffn_kept = chip_halves(after(grad_ffn_low, middle_part), core)
    down_sent = matmul(ffn_sent, inner_low).astype(bf16)
    down_came = to_core(down_sent)
    wide_half = (matmul(middle_kept, grad_wide_low) + wide_came.astype(f32)).astype(bf16)
    wide_own, wide_ring = ring_one(wide_half, "zx", z, x)
    down_half = (matmul(ffn_kept, inner_low) + down_came.astype(f32)).astype(bf16)
    down_own, down_ring = ring_one(down_half, "xz", z, x)
    grad_middle = tensor_sum(
        middle_part, tensor, (wide_sent, down_sent), (wide_half, down_half)
    ).astype(f32)

    grad_hidden_norm, grad_gain_middle = middle_pull(grad_middle)
    grad_hidden = grad_out + grad_hidden_norm
    grad_mixer, grad_gain_mixer = mixer_pull(grad_hidden)
    grad_mixer_low = grad_mixer.astype(bf16)
    grad_mixed_low = matmul(grad_mixer_low, w_mixer[:, :head_dim]).astype(bf16)

    grad_query_rot, grad_kv, to_other = attend_back(
        query_low, key_all, value_all, grad_mixed_low, log_total, query_places, key_row
    )
    from_other = to_context(to_other)
    grad_query_raw, grad_gain_query = query_pull(grad_query_rot)
    grad_kv = grad_kv + from_other.astype(f32)

    def key_shape(raw_rows, gain_vec):
        return rotated(normed(raw_rows, gain_vec), angles)

    key_unused, key_pull = jax.vjp(key_shape, key_raw[:rows], gain_key)
    grad_key_raw, grad_gain_key = key_pull(grad_kv[:, :head_dim])
    grad_qkv_low = jnp.concatenate(
        [grad_query_raw, grad_key_raw, grad_kv[:, head_dim:]], axis=1
    ).astype(bf16)
    input_part = matmul_nt(grad_qkv_low, w_qkv)
    unused, grad_gain_in = input_pull(input_part)
    def narrow(vec):
        return jnp.pad(vec.reshape(32, 8), ((0, 0), (0, 28))).reshape(width)

    columns = jnp.stack(
        [
            grad_gain_in,
            narrow(grad_gain_query),
            narrow(grad_gain_key),
            grad_gain_mixer * 0.25,
            grad_gain_middle * 0.25,
            grad_gain_output * 0.25,
        ]
    )
    columns = jnp.pad(columns, ((0, 128 - 6), (0, 0)))
    input_low = input_part.astype(bf16)
    mixer_sent, mixer_kept = chip_halves(grad_mixer_low, core)
    column_sent, column_kept = chip_halves(columns, core)

    def small_half(normed_rows, column_rows, mixer_rows):
        parts = [matmul(normed_rows, grad_qkv_low), column_rows, matmul(mixer_rows, mixed_low)]
        return jnp.concatenate(parts, axis=1)

    small_sent = small_half(normed_sent, column_sent, mixer_sent).astype(bf16)
    small_came = to_core(small_sent)
    small_own = small_half(normed_kept, column_kept, mixer_kept)
    small_half_sum = (small_own + small_came.astype(f32)).astype(bf16)
    small_ring_own, small_ring = ring_one(small_half_sum, "xz", z, x)
    wide_part = ring_total(wide_own, [after(p, to_other) for p in wide_ring]).astype(bf16)
    wide_two = ring_two(wide_part, "zx", z, x)
    down_part = ring_total(down_own, [after(p, to_other) for p in down_ring]).astype(bf16)
    down_two = ring_two(down_part, "xz", z, x)
    grad_normed = tensor_sum(
        input_low, tensor, (small_sent,), (wide_part, down_part, *small_ring)
    ).astype(f32)
    small_part = ring_total(small_ring_own, small_ring).astype(bf16)
    small = owned(*ring_two(small_part, "xz", z, x), x_lo)
    wide_out = owned(*wide_two, x_lo)
    down_out = owned(*down_two, x_lo)[:, :hidden].T
    gate_out, up_out = wide_out[:, :hidden], wide_out[:, padded : padded + hidden]
    query_out = small[:, :head_dim]
    shared = small[:, head_dim : 3 * head_dim + 128]
    mixer_out = small[:, 3 * head_dim + 128 :].T
    shared_low = jnp.pad(shared, ((0, 4), (0, 0))).astype(bf16)
    for piece in [along_y(shared_low, step) for step in STEPS]:
        shared = shared + piece[:36].astype(f32)
    kv_out = lax.dynamic_slice_in_dim(shared[:, : 2 * head_dim], 9 * tensor, 9, 0)
    key_out, value_out = kv_out[:, :head_dim], kv_out[:, head_dim:]
    gain_cols = shared[:, 2 * head_dim :]
    two = lax.dynamic_slice_in_dim(gain_cols, 2 * tensor, 2, 0)

    grad_resid_norm, unused_gain = input_pull(grad_normed)
    grad_input = grad_hidden + grad_resid_norm
    return (
        output,
        grad_input,
        query_out,
        key_out,
        value_out,
        mixer_out,
        gate_out,
        up_out,
        down_out,
        gain_cols[:, 0],
        two[:, 1],
        two[:, 2],
        gain_cols[:, 3],
        gain_cols[:, 4],
        gain_cols[:, 5],
    )


def solution(mesh):
    in_specs = (
        P(("weight", "context"), None),
        P(("weight", "context")),
        P("weight", "tensor"),
        P("weight", None),
        P("weight", None),
        P("tensor", "weight"),
        P("weight", "tensor"),
        P("weight", "tensor"),
        P("tensor", "weight"),
        P("weight"),
        P("weight"),
        P("weight"),
        P("weight"),
        P("weight"),
        P("weight"),
        P(("weight", "context"), None),
    )
    out_specs = (
        P(("weight", "context"), None),
        P(("weight", "context"), None),
        P(("weight", "context"), "tensor"),
        P(("weight", "context", "tensor"), None),
        P(("weight", "context", "tensor"), None),
        P("tensor", ("weight", "context")),
        P(("weight", "context"), "tensor"),
        P(("weight", "context"), "tensor"),
        P("tensor", ("weight", "context")),
        P(("weight", "context")),
        P(("weight", "context", "tensor")),
        P(("weight", "context", "tensor")),
        P(("weight", "context")),
        P(("weight", "context")),
        P(("weight", "context")),
    )
    return jax.shard_map(local, mesh=mesh, in_specs=in_specs, out_specs=out_specs, check_vma=False)
```
